32 devices in a mesh: groups: 2 (over y), rep: 4 (over x, core), tp: 4 (over z).
Axes of the slice: x: 2, y: 2, z: 4, core: 2. Of those that a mesh axis runs over, the one named last changes fastest.
Arguments:
- queries: bfloat16 [2048, 4096], P(('groups', 'rep'), 'tp'), parts along dimension 0, may hold values from -4.5 to 4.5
- keys: bfloat16 [16, 3200, 4, 128], P(('groups', 'rep'), 'tp'), parts along dimension 0, may hold values from -4.5 to 4.5
- values: bfloat16 [16, 3200, 4, 128], P(('groups', 'rep'), 'tp'), parts along dimension 0, may hold values from -24 to 24
- lengths: int32 [16], P(('groups', 'rep')), parts along dimension 0, may hold values from 1 to 128, as said below
- offsets: int32 [16], P(('groups', 'rep')), parts along dimension 0, may hold values from 0 to 3072, as said below
- tenants: int32 [16], P(('groups', 'rep')), parts along dimension 0, may hold values from 0 to 127
- tenant_storage_rows: int32 [128], replicated, may hold values from 0 to 127, each once
- output_weight: bfloat16 [4096, 5120], P(None, 'tp'), may hold values from -0.09375 to 0.09375
- adapter_down_factors: bfloat16 [128, 64, 4096], P(None, 'rep', 'tp'), may hold values from -0.09375 to 0.09375
- adapter_up_factors: bfloat16 [128, 64, 5120], P(None, 'rep', 'tp'), may hold values from -0.75 to 0.75
Outputs:
- mixed: bfloat16 [2048, 5120], P(('groups', 'rep'), 'tp'), parts along dimension 0
The draws below stay inside these ranges and needn't reach their ends.
There are 2 independent parts, one for each index of `groups`. The reference program is written for one: setup_inputs(seed, part) draws one part's arguments, and reference() takes and returns one part's arrays. A program takes and returns all parts, laid end to end along the dimension named above; an argument that names none is the same for every part. Nothing has to cross between parts.
Inputs may be any that keep to these rules, and one draw needn't show every extreme that they name: `lengths`: some block has exactly 128 new rows and some block exactly one. offsets[b] + lengths[b] <= 3200 for every block; some block reaches 3200 with 128 new rows, and some block starts at 0. `tenants`: several blocks may share a tenant. `tenant_storage_rows`: every storage row once.
All inputs are finite; a program needn't handle non-finite values.
Results may differ from the reference program's by a relative error of at most 0.0061.
Values may be sent and summed in bfloat16 or wider, within the bound.
A program may use at most 128 MiB of HBM per device.

```python
import math
import jax
import jax.numpy as jnp
import numpy as np
from jax import lax

MODEL_WIDTH = 5120
QUERY_HEADS = 32
KVH = 4
HEAD_SIZE = 128
ADAPTER_RANK = 64
BLOCK = 128
CTX = 3200
STORED_ADAPTERS = 128
BLOCKS = 8
TOKENS = 1024


def block_spans(key):
    span_key = jax.random.fold_in(key, 501)
    first_key, second_key, third_key = jax.random.split(span_key, 3)
    block_ids = jnp.arange(BLOCKS, dtype=jnp.int32)
    full_block = jax.random.randint(second_key, (), 0, BLOCKS)
    drawn_lengths = jax.random.randint(first_key, (BLOCKS,), 1, BLOCK + 1)
    drawn_lengths = jnp.where(block_ids == full_block, BLOCK, drawn_lengths)
    drawn_lengths = jnp.where(block_ids == (full_block + 2) % BLOCKS, 1, drawn_lengths)
    drawn_offsets = jax.random.randint(third_key, (BLOCKS,), 0, CTX - BLOCK + 1)
    drawn_offsets = jnp.where(block_ids == full_block, CTX - BLOCK, drawn_offsets)
    drawn_offsets = jnp.where(block_ids == (full_block + 1) % BLOCKS, 0, drawn_offsets)
    return (drawn_lengths.astype(jnp.int32), drawn_offsets.astype(jnp.int32))


def draw_lengths(key, part):
    return block_spans(key)[0]


def draw_offsets(key, part):
    return block_spans(key)[1]


def draw_queries(key, part):
    key = jax.random.fold_in(key, 11)
    drawn = jnp.clip(jax.random.normal(key, (BLOCKS, BLOCK, QUERY_HEADS, HEAD_SIZE), jnp.float32), -4.5, 4.5)
    return drawn.reshape(TOKENS, QUERY_HEADS * HEAD_SIZE).astype(jnp.bfloat16)


def draw_keys(key, part):
    key = jax.random.fold_in(key, 12)
    drawn = jnp.clip(jax.random.normal(key, (BLOCKS, CTX, KVH, HEAD_SIZE), jnp.float32), -4.5, 4.5)
    return drawn.astype(jnp.bfloat16)


def plant(values, own_key, smallest, largest):
    longest = values.shape.index(max(values.shape))
    spots = []
    for shift in (0, 1):
        where = [jax.random.randint(jax.random.fold_in(own_key, axis), (), 0, length) for axis, length in enumerate(values.shape)]
        where[longest] = (where[longest] + shift) % values.shape[longest]
        spots.append(tuple(where))
    return values.at[spots[0]].set(smallest).at[spots[1]].set(largest)


def level_of(stream_key, extent, cuts, low, largest):
    loudness = 1.0
    for position, blocks in cuts:
        draws = jax.random.uniform(jax.random.fold_in(jax.random.fold_in(stream_key, 6), position), (blocks,), jnp.float32, low / len(cuts), largest / len(cuts))
        loudness = loudness * jnp.repeat(jnp.exp(draws), extent[position] // blocks).reshape((-1,) + (1,) * (len(extent) - 1 - position))
    return loudness


def rank_bounds(number_of, slope):
    portions = [(1 << 20) // math.isqrt(rank ** slope) + 1 for rank in range(1, number_of + 1)]
    scale = 1 + sum(portions) // (1 << 30)
    return np.cumsum(np.array([max(1, weight // scale) for weight in portions]))


def ranked_ids(key, extent, count, slope):
    table = rank_bounds(count, slope)
    pick = jax.random.randint(jax.random.fold_in(key, 1), extent, 0, int(table[count - 1]))
    standing = jnp.searchsorted(jnp.asarray(table, jnp.int32), pick, side="right")
    return jax.random.permutation(jax.random.fold_in(key, 2), count)[standing].astype(jnp.int32)


def bell_draw(rng, shape, scale, reach, cuts=(), kind=jnp.bfloat16):
    level = level_of(rng, shape, cuts, -0.22, 0.18) if cuts else 1.0
    values = jax.random.normal(rng, shape, jnp.float32) * scale * level
    return jnp.minimum(jnp.maximum(values, -reach), reach).astype(kind)


def setup_inputs(seed: int = 0, part: int = 0) -> dict:
    key_list = jax.random.split(jax.random.key(seed), 11)
    part_splits = jax.random.split(jax.random.fold_in(key_list[10], part), 11)
    queries = draw_queries(jax.random.fold_in(jax.random.fold_in(key_list[10], part), 71), part)
    keys = draw_keys(jax.random.fold_in(jax.random.fold_in(key_list[10], part), 71), part)
    values = bell_draw(part_splits[2], (BLOCKS, CTX, KVH, HEAD_SIZE), 4.0, 24.0, ((0, 4), (1, 4)))
    lengths = draw_lengths(jax.random.fold_in(jax.random.fold_in(key_list[10], part), 71), part)
    offsets = draw_offsets(jax.random.fold_in(jax.random.fold_in(key_list[10], part), 71), part)
    tenants = plant(ranked_ids(part_splits[5], (BLOCKS,), STORED_ADAPTERS, 2), jax.random.fold_in(part_splits[5], 3), 0, STORED_ADAPTERS - 1).astype(jnp.int32)
    tenant_storage_rows = jax.random.permutation(key_list[6], STORED_ADAPTERS).astype(jnp.int32)
    output_weight = bell_draw(key_list[7], (QUERY_HEADS * HEAD_SIZE, MODEL_WIDTH), (QUERY_HEADS * HEAD_SIZE) ** -0.5, 0.09375, ((1, 4),))
    adapter_down_factors = bell_draw(key_list[8], (STORED_ADAPTERS, ADAPTER_RANK, QUERY_HEADS * HEAD_SIZE), (QUERY_HEADS * HEAD_SIZE) ** -0.5, 0.09375, ((1, 4), (2, 4)))
    adapter_up_factors = bell_draw(key_list[9], (STORED_ADAPTERS, ADAPTER_RANK, MODEL_WIDTH), ADAPTER_RANK ** -0.5, 0.75, ((1, 4), (2, 4)))
    return {"queries": queries, "keys": keys, "values": values, "lengths": lengths, "offsets": offsets, "tenants": tenants, "tenant_storage_rows": tenant_storage_rows, "output_weight": output_weight, "adapter_down_factors": adapter_down_factors, "adapter_up_factors": adapter_up_factors}


def reference(queries, keys, values, lengths, offsets, tenants, tenant_storage_rows, output_weight, adapter_down_factors, adapter_up_factors):
    group_size = QUERY_HEADS // KVH
    score_scale = 1.0 / math.sqrt(HEAD_SIZE)
    row_ids = jnp.arange(BLOCK, dtype=jnp.int32)
    position_ids = jnp.arange(CTX, dtype=jnp.int32)
    blocks_of_queries = queries.reshape(BLOCKS, BLOCK, KVH, group_size, HEAD_SIZE)

    def one_block(block_items):
        query_block, key_block, value_block, length, offset = block_items
        scores = jnp.einsum('qgrd,kgd->grqk', query_block.astype(jnp.float32), key_block.astype(jnp.float32)) * score_scale
        visible = position_ids[None, :] <= offset + row_ids[:, None]
        scores = jnp.where(visible[None, None], scores, -1e+30)
        top_score = lax.optimization_barrier(jnp.max(scores, axis=-1, keepdims=True))
        weights = jnp.exp(scores - top_score)
        probabilities = (weights / lax.optimization_barrier(jnp.sum(weights, axis=-1, keepdims=True))).astype(jnp.bfloat16)
        projected_output = jnp.einsum('grqk,kgd->qgrd', probabilities.astype(jnp.float32), value_block.astype(jnp.float32))
        projected_output = jnp.where((row_ids < length)[:, None, None, None], projected_output, 0.0)
        return projected_output.astype(jnp.bfloat16).reshape(BLOCK, QUERY_HEADS * HEAD_SIZE)
    attended = lax.map(one_block, (blocks_of_queries, keys, values, lengths, offsets)).reshape(TOKENS, QUERY_HEADS * HEAD_SIZE)
    base = jnp.dot(attended, output_weight, preferred_element_type=jnp.float32)
    storage_slot_rows = tenant_storage_rows[tenants]
    down_factor_rows = adapter_down_factors[storage_slot_rows]
    up_factor_rows = adapter_up_factors[storage_slot_rows]
    attended_blocks = attended.reshape(BLOCKS, BLOCK, QUERY_HEADS * HEAD_SIZE)
    rank_product = jnp.einsum('bqw,brw->bqr', attended_blocks.astype(jnp.float32), down_factor_rows.astype(jnp.float32)).astype(jnp.bfloat16)
    adapter_delta = jnp.einsum('pmx,pxy->pmy', rank_product.astype(jnp.float32), up_factor_rows.astype(jnp.float32))
    mixed = base.reshape(BLOCKS, BLOCK, MODEL_WIDTH) + adapter_delta
    return mixed.astype(jnp.bfloat16).reshape(TOKENS, MODEL_WIDTH)
```

```python
import functools
import math

import jax
import jax.numpy as jnp
from jax import lax
from jax.experimental import pallas as pl
from jax.experimental.pallas import tpu as pltpu
from jax.sharding import PartitionSpec as P

MESH = pl.DeviceIdType.MESH


def kernel(
    n,
    reps,
    copies,
    chunk,
    kept,
    off_ref,
    len_ref,
    q_ref,
    k_hbm,
    v_hbm,
    w_hbm,
    down_hbm,
    up_hbm,
    o_ref,
    kbuf,
    vbuf,
    probs,
    rows_all,
    low_all,
    dbuf,
    ubuf,
    wbuf,
    kv_send,
    kv_recv,
    own_sem,
    w_sem,
    ad_send,
    ad_recv,
    ad_own,
    row_send,
    row_recv,
    low_send,
    low_recv,
):
    blocks = k_hbm.shape[0]
    padded = k_hbm.shape[1]
    hd = kbuf.shape[-1]
    block_rows = q_ref.shape[0] // blocks
    width = q_ref.shape[1]
    heads = width // hd
    me = lax.axis_index("tp")
    my_rep = lax.axis_index("rep")

    def peer(d):
        return lax.rem(me + d, n)

    def source(d):
        return lax.rem(me + n - d, n)

    def rpeer(d):
        return lax.rem(my_rep + d, reps)

    def rsource(d):
        return lax.rem(my_rep + reps - d, reps)

    barrier = pltpu.get_barrier_semaphore()
    for d in range(1, n):
        pl.semaphore_signal(barrier, inc=1, device_id={"tp": peer(d)}, device_id_type=MESH)
    for d in range(1, reps):
        pl.semaphore_signal(barrier, inc=1, device_id={"rep": rpeer(d)}, device_id_type=MESH)
    pl.semaphore_wait(barrier, n - 1 + reps - 1)

    hbms = (k_hbm, v_hbm)
    bufs = (kbuf, vbuf)

    def columns(t):
        return pl.ds(pl.multiple_of((t // copies) * hd, hd), hd)

    def span(t):
        return pl.ds(pl.multiple_of(t * padded, 16), padded)

    def kv_copy(b, kind, d, slot, to):
        return pltpu.make_async_remote_copy(
            src_ref=hbms[kind].at[b, :, columns(to)],
            dst_ref=bufs[kind].at[b, span(slot)],
            send_sem=kv_send.at[b, kind, d],
            recv_sem=kv_recv.at[b, kind, d],
            device_id={"tp": to},
            device_id_type=MESH,
        )

    def kv_own(b, kind):
        return pltpu.make_async_copy(
            hbms[kind].at[b, :, columns(me)], bufs[kind].at[b, span(me)], own_sem.at[b, kind]
        )

    def ad_copy(which, d, slot, to):
        src, dst = ((down_hbm, dbuf), (up_hbm, ubuf))[which]
        return pltpu.make_async_remote_copy(
            src_ref=src.at[to],
            dst_ref=dst.at[slot],
            send_sem=ad_send.at[which, d],
            recv_sem=ad_recv.at[which, d],
            device_id={"rep": to},
            device_id_type=MESH,
        )

    def ad_self(which):
        src, dst = ((down_hbm, dbuf), (up_hbm, ubuf))[which]
        return pltpu.make_async_copy(src.at[my_rep], dst.at[my_rep], ad_own.at[which])

    def row_copy(b, d, slot, to):
        return pltpu.make_async_remote_copy(
            src_ref=rows_all.at[slot, b],
            dst_ref=rows_all.at[slot, b],
            send_sem=row_send.at[b, d],
            recv_sem=row_recv.at[b, d],
            device_id={"tp": to},
            device_id_type=MESH,
        )

    def low_copy(b, d, slot, to):
        return pltpu.make_async_remote_copy(
            src_ref=low_all.at[slot, b],
            dst_ref=low_all.at[slot, b],
            send_sem=low_send.at[b, d],
            recv_sem=low_recv.at[b, d],
            device_id={"tp": to},
            device_id_type=MESH,
        )

    for b in range(blocks):
        for kind in range(2):
            for d in range(1, n):
                kv_copy(b, kind, d, me, peer(d)).start()
            kv_own(b, kind).start()
    for which in range(2):
        for d in range(1, reps):
            ad_copy(which, d, my_rep, rpeer(d)).start()
        ad_self(which).start()
    w_copy = pltpu.make_async_copy(w_hbm, wbuf, w_sem)
    w_copy.start()

    def kv_wait(b, kind):
        kv_own(b, kind).wait()
        for d in range(1, n):
            kv_copy(b, kind, d, source(d), peer(d)).wait_recv()

    scale = 1.0 / math.sqrt(hd)
    group = 2 if heads % 2 == 0 else 1
    total = n * padded

    def weigh(b):
        row = lax.rem(
            lax.broadcasted_iota(jnp.int32, (group * block_rows, 1), 0), jnp.int32(block_rows)
        )
        col = lax.broadcasted_iota(jnp.int32, (1, total), 1)
        if padded != chunk:
            part = col // padded
            inner = col - part * padded
            col = jnp.where(inner < chunk, part * chunk + inner, jnp.int32(1 << 30))
        limit = row + off_ref[b]

        @pl.loop(0, heads // group)
        def _(g):
            pieces = [
                q_ref[
                    pl.ds(b * block_rows, block_rows),
                    pl.ds(pl.multiple_of((g * group + j) * hd, hd), hd),
                ]
                for j in range(group)
            ]
            q = jnp.concatenate(pieces, axis=0)
            s = lax.dot_general(
                q, kbuf[b], (((1,), (1,)), ((), ())), preferred_element_type=jnp.float32
            )
            s = jnp.where(col <= limit, s * scale, -1e30)
            e = jnp.exp(s - jnp.max(s, axis=1, keepdims=True))
            inv = 1.0 / jnp.sum(e, axis=1, keepdims=True)
            probs[g] = (e * inv).astype(jnp.bfloat16)

    def gather_values(b):
        row = lax.broadcasted_iota(jnp.int32, (block_rows, 1), 0)
        live = row < len_ref[b]

        @pl.loop(0, heads // group)
        def _(g):
            o = jnp.dot(probs[g], vbuf[b], preferred_element_type=jnp.float32)
            for j in range(group):
                piece = jnp.where(live, o[j * block_rows : (j + 1) * block_rows], 0.0)
                rows_all[
                    me, b, :, pl.ds(pl.multiple_of((g * group + j) * hd, hd), hd)
                ] = piece.astype(jnp.bfloat16)

    rank_part = dbuf.shape[2]

    def lower(b):
        for r in range(reps):
            low_all[me, b, r * rank_part : (r + 1) * rank_part, :] = lax.dot_general(
                dbuf[r, b],
                rows_all[me, b],
                (((1,), (1,)), ((), ())),
                preferred_element_type=jnp.float32,
            )

    for b in range(blocks):
        kv_wait(b, 0)
        weigh(b)
        kv_wait(b, 1)
        gather_values(b)
        for d in range(1, n):
            row_copy(b, d, me, peer(d)).start()
        if b == 0:
            for which in range(2):
                ad_self(which).wait()
                for d in range(1, reps):
                    ad_copy(which, d, rsource(d), rpeer(d)).wait_recv()
        lower(b)
        for d in range(1, n):
            low_copy(b, d, me, peer(d)).start()

    w_copy.wait()
    for b in range(blocks):

        def project(t):
            return jnp.dot(
                rows_all[t, b],
                wbuf[pl.ds(pl.multiple_of(t * width, width), width), :],
                preferred_element_type=jnp.float32,
            )

        acc = project(me)
        low = low_all[me, b]
        for d in range(1, n):
            row_copy(b, d, source(d), peer(d)).wait_recv()
            acc += project(source(d))
        for d in range(1, n):
            low_copy(b, d, source(d), peer(d)).wait_recv()
            low += low_all[source(d), b]
        low = low.astype(jnp.bfloat16)
        for r in range(reps):
            acc += lax.dot_general(
                low[r * rank_part : (r + 1) * rank_part],
                ubuf[r, b],
                (((0,), (0,)), ((), ())),
                preferred_element_type=jnp.float32,
            )
        o_ref[b * block_rows : (b + 1) * block_rows, :] = acc.astype(o_ref.dtype)

    for b in range(blocks):
        for d in range(1, n):
            for kind in range(2):
                kv_copy(b, kind, d, me, peer(d)).wait_send()
            row_copy(b, d, me, peer(d)).wait_send()
            low_copy(b, d, me, peer(d)).wait_send()
    for which in range(2):
        for d in range(1, reps):
            ad_copy(which, d, my_rep, rpeer(d)).wait_send()


def on_device(
    queries,
    keys,
    values,
    lengths,
    offsets,
    tenants,
    tenant_storage_rows,
    output_weight,
    adapter_down_factors,
    adapter_up_factors,
):
    n = lax.axis_size("tp")
    reps = lax.axis_size("rep")
    blocks, chunk, kv_heads, hd = keys.shape
    row_count, width = queries.shape
    block_rows = row_count // blocks
    copies = n // kv_heads
    out_width = output_weight.shape[1]
    rank_part = adapter_down_factors.shape[1]
    kept = kv_heads * hd

    all_tenants = lax.all_gather(tenants, "rep", axis=0, tiled=True)
    catalog = jnp.arange(tenant_storage_rows.shape[0], dtype=jnp.int32)
    slots = jnp.sum(
        jnp.where(all_tenants[:, None] == catalog[None, :], tenant_storage_rows[None, :], 0), axis=1
    )
    selected_down = jnp.take(adapter_down_factors, slots, axis=0).reshape(
        reps, blocks, rank_part, adapter_down_factors.shape[2]
    )
    selected_up = jnp.take(adapter_up_factors, slots, axis=0).reshape(
        reps, blocks, rank_part, adapter_up_factors.shape[2]
    )

    flat_keys = keys.reshape(blocks, chunk, kept)
    flat_values = values.reshape(blocks, chunk, kept)
    padded = -(-chunk // 16) * 16
    if padded != chunk:
        extra = ((0, 0), (0, padded - chunk), (0, 0))
        flat_keys = jnp.pad(flat_keys, extra)
        flat_values = jnp.pad(flat_values, extra)

    heads = width // hd
    group = 2 if heads % 2 == 0 else 1
    bf16, f32 = jnp.bfloat16, jnp.float32
    dma = pltpu.SemaphoreType.DMA
    anywhere = pl.BlockSpec(memory_space=pl.ANY)
    smem = pl.BlockSpec(memory_space=pltpu.SMEM)
    vmem = pl.BlockSpec(memory_space=pltpu.VMEM)
    return pl.pallas_call(
        functools.partial(kernel, n, reps, copies, chunk, kept),
        out_shape=jax.ShapeDtypeStruct((row_count, out_width), bf16),
        in_specs=[smem, smem, vmem] + [anywhere] * 5,
        out_specs=vmem,
        scratch_shapes=[
            pltpu.VMEM((blocks, n * padded, hd), bf16),
            pltpu.VMEM((blocks, n * padded, hd), bf16),
            pltpu.VMEM((heads // group, group * block_rows, n * padded), bf16),
            pltpu.VMEM((n, blocks, block_rows, width), bf16),
            pltpu.VMEM((n, blocks, reps * rank_part, block_rows), f32),
            pltpu.VMEM((reps, blocks, rank_part, width), bf16),
            pltpu.VMEM((reps, blocks, rank_part, out_width), bf16),
            pltpu.VMEM((n * width, out_width), bf16),
            dma((blocks, 2, n)),
            dma((blocks, 2, n)),
            dma((blocks, 2)),
            dma,
            dma((2, reps)),
            dma((2, reps)),
            dma((2,)),
            dma((blocks, n)),
            dma((blocks, n)),
            dma((blocks, n)),
            dma((blocks, n)),
        ],
        compiler_params=pltpu.CompilerParams(
            collective_id=0, has_side_effects=True, vmem_limit_bytes=52 * 1024 * 1024
        ),
        cost_estimate=pl.CostEstimate(
            flops=4 * row_count * width * n * chunk + 2 * row_count * n * width * out_width,
            bytes_accessed=2 * n * width * out_width + 8 * blocks * chunk * kept,
            transcendentals=row_count * heads * n * chunk,
        ),
    )(
        offsets,
        lengths,
        queries,
        flat_keys,
        flat_values,
        output_weight,
        selected_down,
        selected_up,
    )


def solution(mesh):
    return jax.shard_map(
        on_device,
        mesh=mesh,
        in_specs=(
            P(("groups", "rep"), "tp"),
            P(("groups", "rep"), "tp", None, None),
            P(("groups", "rep"), "tp", None, None),
            P(("groups", "rep")),
            P(("groups", "rep")),
            P(("groups", "rep")),
            P(),
            P(None, "tp"),
            P(None, "rep", "tp"),
            P(None, "rep", "tp"),
        ),
        out_specs=P(("groups", "rep"), "tp"),
        check_vma=False,
    )
```

```python
import functools
import math

import jax
import jax.numpy as jnp
from jax import lax
from jax.experimental import pallas as pl
from jax.experimental.pallas import tpu as pltpu
from jax.sharding import PartitionSpec as P

MESH = pl.DeviceIdType.MESH


def kernel(
    n,
    reps,
    copies,
    chunk,
    kept,
    off_ref,
    len_ref,
    storage_ref,
    tenant_ref,
    q_ref,
    k_hbm,
    v_hbm,
    w_hbm,
    down_hbm,
    up_hbm,
    o_ref,
    kbuf,
    vbuf,
    probs,
    rows_all,
    low_all,
    acc,
    tenants_got,
    tenants_smem,
    down_table,
    up_table,
    down_sel,
    up_sel,
    dbuf,
    ubuf,
    wbuf,
    kv_send,
    kv_recv,
    own_sem,
    w_sem,
    ad_send,
    ad_recv,
    ad_own,
    ten_send,
    ten_recv,
    ten_sem,
    table_sem,
    row_send,
    row_recv,
    low_send,
    low_recv,
):
    blocks = k_hbm.shape[0]
    padded = k_hbm.shape[1]
    hd = kbuf.shape[-1]
    block_rows = q_ref.shape[0] // blocks
    width = q_ref.shape[1]
    heads = width // hd
    me = lax.axis_index("tp")
    my_rep = lax.axis_index("rep")

    def peer(d):
        return lax.rem(me + d, n)

    def source(d):
        return lax.rem(me + n - d, n)

    def rpeer(d):
        return lax.rem(my_rep + d, reps)

    def rsource(d):
        return lax.rem(my_rep + reps - d, reps)

    barrier = pltpu.get_barrier_semaphore()
    for d in range(1, n):
        pl.semaphore_signal(barrier, inc=1, device_id={"tp": peer(d)}, device_id_type=MESH)
    for d in range(1, reps):
        pl.semaphore_signal(barrier, inc=1, device_id={"rep": rpeer(d)}, device_id_type=MESH)
    pl.semaphore_wait(barrier, n - 1 + reps - 1)

    hbms = (k_hbm, v_hbm)
    bufs = (kbuf, vbuf)

    def columns(t):
        return pl.ds(pl.multiple_of((t // copies) * hd, hd), hd)

    def span(t):
        return pl.ds(pl.multiple_of(t * padded, 16), padded)

    def kv_copy(b, kind, d, slot, to):
        return pltpu.make_async_remote_copy(
            src_ref=hbms[kind].at[b, :, columns(to)],
            dst_ref=bufs[kind].at[b, span(slot)],
            send_sem=kv_send.at[b, kind, d],
            recv_sem=kv_recv.at[b, kind, d],
            device_id={"tp": to},
            device_id_type=MESH,
        )

    def kv_own(b, kind):
        return pltpu.make_async_copy(
            hbms[kind].at[b, :, columns(me)], bufs[kind].at[b, span(me)], own_sem.at[b, kind]
        )

    def ad_copy(which, d, slot, to):
        src, dst = ((down_sel, dbuf), (up_sel, ubuf))[which]
        return pltpu.make_async_remote_copy(
            src_ref=src.at[to],
            dst_ref=dst.at[slot],
            send_sem=ad_send.at[which, d],
            recv_sem=ad_recv.at[which, d],
            device_id={"rep": to},
            device_id_type=MESH,
        )

    def ad_self(which):
        src, dst = ((down_sel, dbuf), (up_sel, ubuf))[which]
        return pltpu.make_async_copy(src.at[my_rep], dst.at[my_rep], ad_own.at[which])

    def row_copy(b, way, t, slot, to):
        return pltpu.make_async_remote_copy(
            src_ref=rows_all.at[slot, b],
            dst_ref=rows_all.at[slot, b],
            send_sem=row_send.at[b, way, t],
            recv_sem=row_recv.at[b, way, t],
            device_id={"tp": to},
            device_id_type=MESH,
        )

    def sends(t):
        return ((me >= t) & (me < n - 1), (me + t <= n - 1) & (me > 0))

    def gets(t):
        return (me >= t + 1, me + t + 1 <= n - 1)

    def send_rows(b, t):
        up_too, down_too = sends(t)

        @pl.when(up_too)
        def _():
            row_copy(b, 0, t, me - t, me + 1).start()

        @pl.when(down_too)
        def _():
            row_copy(b, 1, t, me + t, me - 1).start()

    def sent_rows(b, t):
        up_too, down_too = sends(t)

        @pl.when(up_too)
        def _():
            row_copy(b, 0, t, me - t, me + 1).wait_send()

        @pl.when(down_too)
        def _():
            row_copy(b, 1, t, me + t, me - 1).wait_send()

    def take_rows(b, t):
        below, above = gets(t)

        @pl.when(below)
        def _():
            row_copy(b, 0, t, me - 1 - t, me - 1).wait_recv()

        @pl.when(above)
        def _():
            row_copy(b, 1, t, me + 1 + t, me + 1).wait_recv()

        if t + 1 <= n - 2:
            send_rows(b, t + 1)

    def tenant_copy(d, slot, to):
        return pltpu.make_async_remote_copy(
            src_ref=tenant_ref,
            dst_ref=tenants_got.at[slot],
            send_sem=ten_send.at[d],
            recv_sem=ten_recv.at[d],
            device_id={"rep": to},
            device_id_type=MESH,
        )

    def low_copy(b, d, slot, to):
        return pltpu.make_async_remote_copy(
            src_ref=low_all.at[slot, b],
            dst_ref=low_all.at[slot, b],
            send_sem=low_send.at[b, d],
            recv_sem=low_recv.at[b, d],
            device_id={"tp": to},
            device_id_type=MESH,
        )

    for d in range(1, reps):
        tenant_copy(d, my_rep, rpeer(d)).start()
    tenant_own = pltpu.make_async_copy(tenant_ref, tenants_got.at[my_rep], ten_sem.at[0])
    tenant_own.start()
    for b in range(blocks):
        for kind in range(2):
            for d in range(1, n):
                kv_copy(b, kind, d, me, peer(d)).start()
            kv_own(b, kind).start()
    tables = [
        pltpu.make_async_copy(down_hbm, down_table, table_sem.at[0]),
        pltpu.make_async_copy(up_hbm, up_table, table_sem.at[1]),
    ]
    for copy in tables:
        copy.start()
    w_copy = pltpu.make_async_copy(w_hbm, wbuf, w_sem)
    w_copy.start()

    tenant_own.wait()
    for d in range(1, reps):
        tenant_copy(d, rsource(d), rpeer(d)).wait_recv()
    to_smem = pltpu.make_async_copy(tenants_got, tenants_smem, ten_sem.at[1])
    to_smem.start()
    to_smem.wait()
    for copy in tables:
        copy.wait()
    for r in range(reps):
        for b in range(blocks):
            slot = storage_ref[tenants_smem[r, 0, b]]
            down_sel[r, b] = down_table[slot]
            up_sel[r, b] = up_table[slot]
    for which in range(2):
        for d in range(1, reps):
            ad_copy(which, d, my_rep, rpeer(d)).start()
        ad_self(which).start()

    def kv_wait(b, kind):
        kv_own(b, kind).wait()
        for d in range(1, n):
            kv_copy(b, kind, d, source(d), peer(d)).wait_recv()

    scale = 1.0 / math.sqrt(hd)
    group = 2 if heads % 2 == 0 else 1
    total = n * padded

    def weigh(b):
        row = lax.rem(
            lax.broadcasted_iota(jnp.int32, (group * block_rows, 1), 0), jnp.int32(block_rows)
        )
        col = lax.broadcasted_iota(jnp.int32, (1, total), 1)
        if padded != chunk:
            part = col // padded
            inner = col - part * padded
            col = jnp.where(inner < chunk, part * chunk + inner, jnp.int32(1 << 30))
        limit = row + off_ref[b]

        @pl.loop(0, heads // group)
        def _(g):
            pieces = [
                q_ref[
                    pl.ds(b * block_rows, block_rows),
                    pl.ds(pl.multiple_of((g * group + j) * hd, hd), hd),
                ]
                for j in range(group)
            ]
            q = jnp.concatenate(pieces, axis=0)
            s = lax.dot_general(
                q, kbuf[b], (((1,), (1,)), ((), ())), preferred_element_type=jnp.float32
            )
            s = jnp.where(col <= limit, s * scale, -1e30)
            e = jnp.exp(s - jnp.max(s, axis=1, keepdims=True))
            inv = 1.0 / jnp.sum(e, axis=1, keepdims=True)
            probs[g] = (e * inv).astype(jnp.bfloat16)

    def gather_values(b):
        row = lax.broadcasted_iota(jnp.int32, (block_rows, 1), 0)
        live = row < len_ref[b]

        @pl.loop(0, heads // group)
        def _(g):
            o = jnp.dot(probs[g], vbuf[b], preferred_element_type=jnp.float32)
            for j in range(group):
                piece = jnp.where(live, o[j * block_rows : (j + 1) * block_rows], 0.0)
                rows_all[
                    me, b, :, pl.ds(pl.multiple_of((g * group + j) * hd, hd), hd)
                ] = piece.astype(jnp.bfloat16)

    rank_part = dbuf.shape[2]

    def lower(b):
        for r in range(reps):
            low_all[me, b, r * rank_part : (r + 1) * rank_part, :] = lax.dot_general(
                dbuf[r, b],
                rows_all[me, b],
                (((1,), (1,)), ((), ())),
                preferred_element_type=jnp.float32,
            )

    for b in range(blocks):
        kv_wait(b, 0)
        weigh(b)
        if b > 0 and n > 1:
            take_rows(b - 1, 0)
        kv_wait(b, 1)
        gather_values(b)
        send_rows(b, 0)
        if b == 0:
            for which in range(2):
                ad_self(which).wait()
                for d in range(1, reps):
                    ad_copy(which, d, rsource(d), rpeer(d)).wait_recv()
        lower(b)
        for d in range(1, n):
            low_copy(b, d, me, peer(d)).start()

    def project(b, t):
        return jnp.dot(
            rows_all[t, b],
            wbuf[pl.ds(pl.multiple_of(t * width, width), width), :],
            preferred_element_type=jnp.float32,
        )

    w_copy.wait()
    for b in range(blocks):
        acc[b] = project(b, me)
    for t in range(n - 1):
        for b in range(blocks):
            if t > 0 or b == blocks - 1:
                take_rows(b, t)
            below, above = gets(t)

            @pl.when(below)
            def _():
                acc[b] += project(b, me - 1 - t)

            @pl.when(above)
            def _():
                acc[b] += project(b, me + 1 + t)

    for b in range(blocks):
        low = low_all[me, b]
        for d in range(1, n):
            low_copy(b, d, source(d), peer(d)).wait_recv()
            low += low_all[source(d), b]
        low = low.astype(jnp.bfloat16)
        mixed = acc[b]
        for r in range(reps):
            mixed += lax.dot_general(
                low[r * rank_part : (r + 1) * rank_part],
                ubuf[r, b],
                (((0,), (0,)), ((), ())),
                preferred_element_type=jnp.float32,
            )
        o_ref[b * block_rows : (b + 1) * block_rows, :] = mixed.astype(o_ref.dtype)

    for b in range(blocks):
        for d in range(1, n):
            for kind in range(2):
                kv_copy(b, kind, d, me, peer(d)).wait_send()
            low_copy(b, d, me, peer(d)).wait_send()
        for t in range(n - 1):
            sent_rows(b, t)
    for d in range(1, reps):
        tenant_copy(d, my_rep, rpeer(d)).wait_send()
    for which in range(2):
        for d in range(1, reps):
            ad_copy(which, d, my_rep, rpeer(d)).wait_send()


def on_device(
    queries,
    keys,
    values,
    lengths,
    offsets,
    tenants,
    tenant_storage_rows,
    output_weight,
    adapter_down_factors,
    adapter_up_factors,
):
    n = lax.axis_size("tp")
    reps = lax.axis_size("rep")
    blocks, chunk, kv_heads, hd = keys.shape
    row_count, width = queries.shape
    block_rows = row_count // blocks
    copies = n // kv_heads
    out_width = output_weight.shape[1]
    rank_part = adapter_down_factors.shape[1]
    kept = kv_heads * hd

    stored = adapter_down_factors.shape[0]
    tenant_tile = jnp.pad(tenants[None, :], ((0, 7), (0, 128 - blocks)))

    flat_keys = keys.reshape(blocks, chunk, kept)
    flat_values = values.reshape(blocks, chunk, kept)
    padded = -(-chunk // 16) * 16
    if padded != chunk:
        extra = ((0, 0), (0, padded - chunk), (0, 0))
        flat_keys = jnp.pad(flat_keys, extra)
        flat_values = jnp.pad(flat_values, extra)

    heads = width // hd
    group = 2 if heads % 2 == 0 else 1
    bf16, f32 = jnp.bfloat16, jnp.float32
    dma = pltpu.SemaphoreType.DMA
    anywhere = pl.BlockSpec(memory_space=pl.ANY)
    smem = pl.BlockSpec(memory_space=pltpu.SMEM)
    vmem = pl.BlockSpec(memory_space=pltpu.VMEM)
    return pl.pallas_call(
        functools.partial(kernel, n, reps, copies, chunk, kept),
        out_shape=jax.ShapeDtypeStruct((row_count, out_width), bf16),
        in_specs=[smem, smem, smem, vmem, vmem] + [anywhere] * 5,
        out_specs=vmem,
        scratch_shapes=[
            pltpu.VMEM((blocks, n * padded, hd), bf16),
            pltpu.VMEM((blocks, n * padded, hd), bf16),
            pltpu.VMEM((heads // group, group * block_rows, n * padded), bf16),
            pltpu.VMEM((n, blocks, block_rows, width), bf16),
            pltpu.VMEM((n, blocks, reps * rank_part, block_rows), f32),
            pltpu.VMEM((blocks, block_rows, out_width), f32),
            pltpu.VMEM((reps, 8, 128), jnp.int32),
            pltpu.SMEM((reps, 8, 128), jnp.int32),
            pltpu.VMEM((stored, rank_part, width), bf16),
            pltpu.VMEM((stored, rank_part, out_width), bf16),
            pltpu.VMEM((reps, blocks, rank_part, width), bf16),
            pltpu.VMEM((reps, blocks, rank_part, out_width), bf16),
            pltpu.VMEM((reps, blocks, rank_part, width), bf16),
            pltpu.VMEM((reps, blocks, rank_part, out_width), bf16),
            pltpu.VMEM((n * width, out_width), bf16),
            dma((blocks, 2, n)),
            dma((blocks, 2, n)),
            dma((blocks, 2)),
            dma,
            dma((2, reps)),
            dma((2, reps)),
            dma((2,)),
            dma((reps,)),
            dma((reps,)),
            dma((2,)),
            dma((2,)),
            dma((blocks, 2, n)),
            dma((blocks, 2, n)),
            dma((blocks, n)),
            dma((blocks, n)),
        ],
        compiler_params=pltpu.CompilerParams(
            collective_id=0, has_side_effects=True, vmem_limit_bytes=52 * 1024 * 1024
        ),
        cost_estimate=pl.CostEstimate(
            flops=4 * row_count * width * n * chunk + 2 * row_count * n * width * out_width,
            bytes_accessed=2 * n * width * out_width + 8 * blocks * chunk * kept,
            transcendentals=row_count * heads * n * chunk,
        ),
    )(
        offsets,
        lengths,
        tenant_storage_rows,
        tenant_tile,
        queries,
        flat_keys,
        flat_values,
        output_weight,
        adapter_down_factors,
        adapter_up_factors,
    )


def solution(mesh):
    return jax.shard_map(
        on_device,
        mesh=mesh,
        in_specs=(
            P(("groups", "rep"), "tp"),
            P(("groups", "rep"), "tp", None, None),
            P(("groups", "rep"), "tp", None, None),
            P(("groups", "rep")),
            P(("groups", "rep")),
            P(("groups", "rep")),
            P(),
            P(None, "tp"),
            P(None, "rep", "tp"),
            P(None, "rep", "tp"),
        ),
        out_specs=P(("groups", "rep"), "tp"),
        check_vma=False,
    )
```

```python
import functools
import math

import jax
import jax.numpy as jnp
from jax import lax
from jax.experimental import pallas as pl
from jax.experimental.pallas import tpu as pltpu
from jax.sharding import PartitionSpec as P

MESH = pl.DeviceIdType.MESH


def kernel(
    n,
    reps,
    copies,
    chunk,
    kept,
    off_ref,
    len_ref,
    storage_ref,
    tenant_ref,
    q_ref,
    k_hbm,
    v_hbm,
    w_hbm,
    down_hbm,
    up_hbm,
    o_ref,
    kbuf,
    vbuf,
    probs,
    rows_all,
    low_all,
    acc,
    tenants_got,
    tenants_smem,
    down_table,
    up_table,
    down_sel,
    up_sel,
    dbuf,
    ubuf,
    wbuf,
    kv_send,
    kv_recv,
    own_sem,
    w_sem,
    ad_send,
    ad_recv,
    ad_own,
    ten_send,
    ten_recv,
    ten_sem,
    table_sem,
    row_send,
    row_recv,
    low_send,
    low_recv,
):
    blocks = k_hbm.shape[0]
    padded = k_hbm.shape[1]
    hd = kbuf.shape[-1]
    block_rows = q_ref.shape[0] // blocks
    width = q_ref.shape[1]
    heads = width // hd
    parts = rows_all.shape[2]
    me = lax.axis_index("tp")
    my_rep = lax.axis_index("rep")

    def peer(d):
        return lax.rem(me + d, n)

    def source(d):
        return lax.rem(me + n - d, n)

    def rpeer(d):
        return lax.rem(my_rep + d, reps)

    def rsource(d):
        return lax.rem(my_rep + reps - d, reps)

    barrier = pltpu.get_barrier_semaphore()
    for d in range(1, n):
        pl.semaphore_signal(barrier, inc=1, device_id={"tp": peer(d)}, device_id_type=MESH)
    for d in range(1, reps):
        pl.semaphore_signal(barrier, inc=1, device_id={"rep": rpeer(d)}, device_id_type=MESH)
    pl.semaphore_wait(barrier, n - 1 + reps - 1)

    hbms = (k_hbm, v_hbm)
    bufs = (kbuf, vbuf)

    def columns(t):
        return pl.ds(pl.multiple_of((t // copies) * hd, hd), hd)

    def span(t):
        return pl.ds(pl.multiple_of(t * padded, 16), padded)

    def kv_copy(b, kind, d, slot, to):
        return pltpu.make_async_remote_copy(
            src_ref=hbms[kind].at[b, :, columns(to)],
            dst_ref=bufs[kind].at[b, span(slot)],
            send_sem=kv_send.at[b, kind, d],
            recv_sem=kv_recv.at[b, kind, d],
            device_id={"tp": to},
            device_id_type=MESH,
        )

    def kv_own(b, kind):
        return pltpu.make_async_copy(
            hbms[kind].at[b, :, columns(me)], bufs[kind].at[b, span(me)], own_sem.at[b, kind]
        )

    def ad_copy(which, d, slot, to):
        src, dst = ((down_sel, dbuf), (up_sel, ubuf))[which]
        return pltpu.make_async_remote_copy(
            src_ref=src.at[to],
            dst_ref=dst.at[slot],
            send_sem=ad_send.at[which, d],
            recv_sem=ad_recv.at[which, d],
            device_id={"rep": to},
            device_id_type=MESH,
        )

    def ad_self(which):
        src, dst = ((down_sel, dbuf), (up_sel, ubuf))[which]
        return pltpu.make_async_copy(src.at[my_rep], dst.at[my_rep], ad_own.at[which])

    def row_copy(b, way, t, part, slot, to):
        return pltpu.make_async_remote_copy(
            src_ref=rows_all.at[slot, b, part],
            dst_ref=rows_all.at[slot, b, part],
            send_sem=row_send.at[b, way, t * parts + part],
            recv_sem=row_recv.at[b, way, t * parts + part],
            device_id={"tp": to},
            device_id_type=MESH,
        )

    def sends(t):
        return ((me >= t) & (me < n - 1), (me + t <= n - 1) & (me > 0))

    def gets(t):
        return (me >= t + 1, me + t + 1 <= n - 1)

    def send_rows(b, t, part):
        up_too, down_too = sends(t)

        @pl.when(up_too)
        def _():
            row_copy(b, 0, t, part, me - t, me + 1).start()

        @pl.when(down_too)
        def _():
            row_copy(b, 1, t, part, me + t, me - 1).start()

    def sent_rows(b, t, part):
        up_too, down_too = sends(t)

        @pl.when(up_too)
        def _():
            row_copy(b, 0, t, part, me - t, me + 1).wait_send()

        @pl.when(down_too)
        def _():
            row_copy(b, 1, t, part, me + t, me - 1).wait_send()

    def take_rows(b, t):
        below, above = gets(t)
        for part in range(parts):

            @pl.when(below)
            def _():
                row_copy(b, 0, t, part, me - 1 - t, me - 1).wait_recv()

            @pl.when(above)
            def _():
                row_copy(b, 1, t, part, me + 1 + t, me + 1).wait_recv()

            if t + 1 <= n - 2:
                send_rows(b, t + 1, part)

    def tenant_copy(d, slot, to):
        return pltpu.make_async_remote_copy(
            src_ref=tenant_ref,
            dst_ref=tenants_got.at[slot],
            send_sem=ten_send.at[d],
            recv_sem=ten_recv.at[d],
            device_id={"rep": to},
            device_id_type=MESH,
        )

    def low_copy(b, d, slot, to):
        return pltpu.make_async_remote_copy(
            src_ref=low_all.at[slot, b],
            dst_ref=low_all.at[slot, b],
            send_sem=low_send.at[b, d],
            recv_sem=low_recv.at[b, d],
            device_id={"tp": to},
            device_id_type=MESH,
        )

    for d in range(1, reps):
        tenant_copy(d, my_rep, rpeer(d)).start()
    tenant_own = pltpu.make_async_copy(tenant_ref, tenants_got.at[my_rep], ten_sem.at[0])
    tenant_own.start()
    def kv_start(b, kind):
        for d in range(1, n):
            kv_copy(b, kind, d, me, peer(d)).start()
        kv_own(b, kind).start()

    for b in range(blocks):
        for kind in range(2):
            kv_start(b, kind)
    tables = [
        pltpu.make_async_copy(down_hbm, down_table, table_sem.at[0]),
        pltpu.make_async_copy(up_hbm, up_table, table_sem.at[1]),
    ]
    for copy in tables:
        copy.start()
    w_copy = pltpu.make_async_copy(w_hbm, wbuf, w_sem)
    w_copy.start()

    tenant_own.wait()
    for d in range(1, reps):
        tenant_copy(d, rsource(d), rpeer(d)).wait_recv()
    to_smem = pltpu.make_async_copy(tenants_got, tenants_smem, ten_sem.at[1])
    to_smem.start()
    to_smem.wait()
    for copy in tables:
        copy.wait()
    for r in range(reps):
        for b in range(blocks):
            slot = storage_ref[tenants_smem[r, 0, b]]
            down_sel[r, b] = down_table[slot]
            up_sel[r, b] = up_table[slot]
    for which in range(2):
        for d in range(1, reps):
            ad_copy(which, d, my_rep, rpeer(d)).start()
        ad_self(which).start()

    def kv_wait(b, kind):
        kv_own(b, kind).wait()
        for d in range(1, n):
            kv_copy(b, kind, d, source(d), peer(d)).wait_recv()

    scale = 1.0 / math.sqrt(hd)
    group = 2 if heads % 2 == 0 else 1
    total = n * padded

    def weigh(b):
        row = lax.rem(
            lax.broadcasted_iota(jnp.int32, (group * block_rows, 1), 0), jnp.int32(block_rows)
        )
        col = lax.broadcasted_iota(jnp.int32, (1, total), 1)
        if padded != chunk:
            part = col // padded
            inner = col - part * padded
            col = jnp.where(inner < chunk, part * chunk + inner, jnp.int32(1 << 30))
        limit = row + off_ref[b]

        @pl.loop(0, heads // group)
        def _(g):
            pieces = [
                q_ref[
                    pl.ds(b * block_rows, block_rows),
                    pl.ds(pl.multiple_of((g * group + j) * hd, hd), hd),
                ]
                for j in range(group)
            ]
            q = jnp.concatenate(pieces, axis=0)
            s = lax.dot_general(
                q, kbuf[b], (((1,), (1,)), ((), ())), preferred_element_type=jnp.float32
            )
            s = jnp.where(col <= limit, s * scale, -1e30)
            e = jnp.exp(s - jnp.max(s, axis=1, keepdims=True))
            inv = 1.0 / jnp.sum(e, axis=1, keepdims=True)
            probs[g] = (e * inv).astype(jnp.bfloat16)

    def gather_values(b, part):
        row = lax.broadcasted_iota(jnp.int32, (block_rows, 1), 0)
        live = row < len_ref[b]
        steps = heads // group // parts

        @pl.loop(0, steps)
        def _(g):
            o = jnp.dot(probs[part * steps + g], vbuf[b], preferred_element_type=jnp.float32)
            for j in range(group):
                piece = jnp.where(live, o[j * block_rows : (j + 1) * block_rows], 0.0)
                rows_all[
                    me, b, part, :, pl.ds(pl.multiple_of((g * group + j) * hd, hd), hd)
                ] = piece.astype(jnp.bfloat16)

    rank_part = dbuf.shape[2]
    share = width // parts

    def lower(b):
        for r in range(reps):
            low_all[me, b, r * rank_part : (r + 1) * rank_part, :] = sum(
                lax.dot_general(
                    dbuf[r, b, :, p * share : (p + 1) * share],
                    rows_all[me, b, p],
                    (((1,), (1,)), ((), ())),
                    preferred_element_type=jnp.float32,
                )
                for p in range(parts)
            )

    for b in range(blocks):
        kv_wait(b, 0)
        weigh(b)
        if b > 0 and n > 1:
            take_rows(b - 1, 0)
        kv_wait(b, 1)
        for part in range(parts):
            gather_values(b, part)
            send_rows(b, 0, part)
        if b == 0:
            for which in range(2):
                ad_self(which).wait()
                for d in range(1, reps):
                    ad_copy(which, d, rsource(d), rpeer(d)).wait_recv()
        lower(b)
        for d in range(1, n):
            low_copy(b, d, me, peer(d)).start()

    def project(b, t):
        return sum(
            jnp.dot(
                rows_all[t, b, p],
                wbuf[pl.ds(pl.multiple_of(t * width + p * share, share), share), :],
                preferred_element_type=jnp.float32,
            )
            for p in range(parts)
        )

    w_copy.wait()
    for b in range(blocks):
        acc[b] = project(b, me)
    for t in range(n - 1):
        for b in range(blocks):
            if t > 0 or b == blocks - 1:
                take_rows(b, t)
            below, above = gets(t)

            @pl.when(below)
            def _():
                acc[b] += project(b, me - 1 - t)

            @pl.when(above)
            def _():
                acc[b] += project(b, me + 1 + t)

    for b in range(blocks):
        low = low_all[me, b]
        for d in range(1, n):
            low_copy(b, d, source(d), peer(d)).wait_recv()
            low += low_all[source(d), b]
        low = low.astype(jnp.bfloat16)
        mixed = acc[b]
        for r in range(reps):
            mixed += lax.dot_general(
                low[r * rank_part : (r + 1) * rank_part],
                ubuf[r, b],
                (((0,), (0,)), ((), ())),
                preferred_element_type=jnp.float32,
            )
        o_ref[b * block_rows : (b + 1) * block_rows, :] = mixed.astype(o_ref.dtype)

    for b in range(blocks):
        for d in range(1, n):
            for kind in range(2):
                kv_copy(b, kind, d, me, peer(d)).wait_send()
            low_copy(b, d, me, peer(d)).wait_send()
        for t in range(n - 1):
            for part in range(parts):
                sent_rows(b, t, part)
    for d in range(1, reps):
        tenant_copy(d, my_rep, rpeer(d)).wait_send()
    for which in range(2):
        for d in range(1, reps):
            ad_copy(which, d, my_rep, rpeer(d)).wait_send()


def on_device(
    queries,
    keys,
    values,
    lengths,
    offsets,
    tenants,
    tenant_storage_rows,
    output_weight,
    adapter_down_factors,
    adapter_up_factors,
):
    n = lax.axis_size("tp")
    reps = lax.axis_size("rep")
    blocks, chunk, kv_heads, hd = keys.shape
    row_count, width = queries.shape
    block_rows = row_count // blocks
    copies = n // kv_heads
    out_width = output_weight.shape[1]
    rank_part = adapter_down_factors.shape[1]
    kept = kv_heads * hd

    stored = adapter_down_factors.shape[0]
    tenant_tile = jnp.pad(tenants[None, :], ((0, 7), (0, 128 - blocks)))

    flat_keys = keys.reshape(blocks, chunk, kept)
    flat_values = values.reshape(blocks, chunk, kept)
    padded = -(-chunk // 16) * 16
    if padded != chunk:
        extra = ((0, 0), (0, padded - chunk), (0, 0))
        flat_keys = jnp.pad(flat_keys, extra)
        flat_values = jnp.pad(flat_values, extra)

    heads = width // hd
    group = 2 if heads % 2 == 0 else 1
    parts = 2 if (heads // group) % 2 == 0 else 1
    bf16, f32 = jnp.bfloat16, jnp.float32
    dma = pltpu.SemaphoreType.DMA
    anywhere = pl.BlockSpec(memory_space=pl.ANY)
    smem = pl.BlockSpec(memory_space=pltpu.SMEM)
    vmem = pl.BlockSpec(memory_space=pltpu.VMEM)
    return pl.pallas_call(
        functools.partial(kernel, n, reps, copies, chunk, kept),
        out_shape=jax.ShapeDtypeStruct((row_count, out_width), bf16),
        in_specs=[smem, smem, smem, vmem, vmem] + [anywhere] * 5,
        out_specs=vmem,
        scratch_shapes=[
            pltpu.VMEM((blocks, n * padded, hd), bf16),
            pltpu.VMEM((blocks, n * padded, hd), bf16),
            pltpu.VMEM((heads // group, group * block_rows, n * padded), bf16),
            pltpu.VMEM((n, blocks, parts, block_rows, width // parts), bf16),
            pltpu.VMEM((n, blocks, reps * rank_part, block_rows), f32),
            pltpu.VMEM((blocks, block_rows, out_width), f32),
            pltpu.VMEM((reps, 8, 128), jnp.int32),
            pltpu.SMEM((reps, 8, 128), jnp.int32),
            pltpu.VMEM((stored, rank_part, width), bf16),
            pltpu.VMEM((stored, rank_part, out_width), bf16),
            pltpu.VMEM((reps, blocks, rank_part, width), bf16),
            pltpu.VMEM((reps, blocks, rank_part, out_width), bf16),
            pltpu.VMEM((reps, blocks, rank_part, width), bf16),
            pltpu.VMEM((reps, blocks, rank_part, out_width), bf16),
            pltpu.VMEM((n * width, out_width), bf16),
            dma((blocks, 2, n)),
            dma((blocks, 2, n)),
            dma((blocks, 2)),
            dma,
            dma((2, reps)),
            dma((2, reps)),
            dma((2,)),
            dma((reps,)),
            dma((reps,)),
            dma((2,)),
            dma((2,)),
            dma((blocks, 2, n * parts)),
            dma((blocks, 2, n * parts)),
            dma((blocks, n)),
            dma((blocks, n)),
        ],
        compiler_params=pltpu.CompilerParams(
            collective_id=0, has_side_effects=True, vmem_limit_bytes=52 * 1024 * 1024
        ),
        cost_estimate=pl.CostEstimate(
            flops=4 * row_count * width * n * chunk + 2 * row_count * n * width * out_width,
            bytes_accessed=2 * n * width * out_width + 8 * blocks * chunk * kept,
            transcendentals=row_count * heads * n * chunk,
        ),
    )(
        offsets,
        lengths,
        tenant_storage_rows,
        tenant_tile,
        queries,
        flat_keys,
        flat_values,
        output_weight,
        adapter_down_factors,
        adapter_up_factors,
    )


def solution(mesh):
    return jax.shard_map(
        on_device,
        mesh=mesh,
        in_specs=(
            P(("groups", "rep"), "tp"),
            P(("groups", "rep"), "tp", None, None),
            P(("groups", "rep"), "tp", None, None),
            P(("groups", "rep")),
            P(("groups", "rep")),
            P(("groups", "rep")),
            P(),
            P(None, "tp"),
            P(None, "rep", "tp"),
            P(None, "rep", "tp"),
        ),
        out_specs=P(("groups", "rep"), "tp"),
        check_vma=False,
    )
```
